128 devices in a mesh: grp: 4 (over y_hi, core), dev: 32 (over x, y_lo, z).
Axes of the slice: x: 4, y: 4 (y_hi: 2, y_lo: 2; y = y_hi * 2 + y_lo), z: 4, core: 2. Of those that a mesh axis runs over, the one named last changes fastest.
Arguments:
- grad_parts: float32 [4, 2, 32, 1024, 1024], P('grp', None, 'dev'), may hold values from -4 to 4
- light_parts: float32 [4, 1024, 1024], P('grp'), may hold values from 0.1 to 1
- object_field: float32 [2, 32, 1024, 1024], P(None, 'dev', 'grp'), may hold values from -4 to 4
Outputs:
- updated: float32 [2, 32, 1024, 1024], P(None, 'dev', 'grp')
The draws below stay inside these ranges and needn't reach their ends.
All inputs are finite; a program needn't handle non-finite values.
Results may differ from the reference program's by a relative error of at most 0.000073.
Values sent between devices are 32-bit elements; how exact they have to be, the bound alone decides.
A program may use at most 128 MiB of HBM per device.

```python
import math
import jax
import jax.numpy as jnp
from jax import lax

S = 32
NX = 1024
NY = 1024
N_GRP = 4


def with_spikes(entries, rng, source, target, parts, factor):
    owner, partner = [(jnp.arange(entries.shape[dim]) // (entries.shape[dim] // parts)).reshape([-1 if axis == dim else 1 for axis in range(entries.ndim)]) for dim in (source, target)]
    chosen = jax.random.permutation(rng, parts)[partner]
    strong = (owner == chosen) | (owner == (partner + parts // 2) % parts)
    return jnp.where(strong, factor * entries, entries)


def steps_of(own_key, dims, pieces, smallest, high):
    loudness, own = 1.0, jax.random.fold_in(own_key, 6)
    for position, shards_of in pieces:
        heights = jnp.exp(jax.random.uniform(jax.random.fold_in(own, position), (shards_of,), jnp.float32, smallest / len(pieces), high / len(pieces)))
        loudness = loudness * jnp.repeat(heights, dims[position] // shards_of).reshape([-1 if axis == position else 1 for axis in range(len(dims))])
    return loudness


def gaussian(own_key, shape, spread, most, split=(), held_as=jnp.bfloat16):
    entries = jax.random.normal(own_key, shape, jnp.float32) * spread
    if len(split) > 0:
        entries = steps_of(own_key, shape, split, -0.22, 0.18) * entries
    return jnp.clip(entries, min=-most, max=most).astype(held_as)


def gaussian_with(own_key, extent, spread, most, shards, heavy, kind=jnp.bfloat16):
    drawn = spread * jax.random.normal(own_key, extent, jnp.float32)
    if shards:
        drawn = drawn * steps_of(own_key, extent, shards, -0.22, 0.18)
    return jnp.clip(with_spikes(drawn, jax.random.fold_in(own_key, 3), *heavy), -most, most).astype(kind)


def setup_inputs(seed: int = 0) -> dict:
    keys = jax.random.split(jax.random.key(seed), 4)
    return {
        "grad_parts": gaussian_with(keys[0], (N_GRP, 2, S, NY, NX), 0.25, 4.0, ((0, 4), (2, 32)), (0, 3, 4, 2.0), jnp.float32),
        "light_parts": jnp.clip(jnp.exp(math.log(1.0) - 2.3025851 * jax.random.uniform(keys[1], (N_GRP, NY, NX), jnp.float32) ** steps_of(keys[1], (N_GRP, NY, NX), ((0, 4),), -0.2, 0.2)), 0.1, 1.0),
        "object_field": gaussian(keys[2], (2, S, NY, NX), 0.6, 4.0, ((1, 32), (2, 4)), jnp.float32),
    }


damping = 0.05
ceiling = 0.4

def depth_taper(count):
    wavenumber = jnp.arange(count, dtype=jnp.int32)
    signed = jnp.where(2 * wavenumber < count, wavenumber, wavenumber - count).astype(jnp.float32)
    return jnp.exp(-(signed / (count / 8.0)) ** 2)

def reference(grad_parts, light_parts, object_field):
    gradient = lax.optimization_barrier(jnp.sum(grad_parts, axis=0))
    lighting = lax.optimization_barrier(jnp.sum(light_parts, axis=0))
    stepped = object_field - gradient / (lighting + damping)
    waves = jnp.fft.fft(lax.complex(stepped[0], stepped[1]), axis=0)
    smooth = jnp.fft.ifft(waves * depth_taper(S)[:, None, None], axis=0)
    real_part = jnp.real(smooth)
    imag_part = jnp.imag(smooth)
    amplitude = jnp.sqrt(real_part * real_part + imag_part * imag_part)
    factor = ceiling / jnp.maximum(amplitude, ceiling)
    return jnp.stack([real_part * factor, imag_part * factor])
```

```python
import functools
import math

import jax
import jax.numpy as jnp
import numpy as np
from jax import lax
from jax.experimental import pallas as pl
from jax.experimental.pallas import tpu as pltpu
from jax.sharding import PartitionSpec as P

damping = 0.05
ceiling = 0.4
MESH = pl.DeviceIdType.MESH
CHUNKS = 4


def mixing_matrix(count, lanes):
    wavenumber = np.arange(count)
    signed = np.where(2 * wavenumber < count, wavenumber, wavenumber - count)
    taper = np.exp(-((signed / (count / 8.0)) ** 2))
    offsets = (wavenumber[:, None] - wavenumber[None, :]) % count
    angles = 2.0 * math.pi / count * ((wavenumber[None, None, :] * offsets[:, :, None]) % count)
    mixing = np.sum(taper * np.cos(angles), axis=2) / count
    return np.kron(mixing, np.eye(lanes)).astype(np.float32)


def wait_for(ref, sem):
    pltpu.make_async_copy(ref, ref, sem).wait()


def kernel(
    mix_ref, grad, light, field, out,
    pbuf, cbuf, obuf, lbuf, dbuf, from_a, from_b, from_d, sbuf, xbuf, ybuf,
    load_sem, field_sem, core_send, core_recv, light_send, light_recv, damp_send, damp_recv,
    y_send, y_recv, plane_send, plane_recv, back_send, back_recv,
):
    width = pbuf.shape[-1]
    g = lax.axis_index("grp")
    me = lax.axis_index("dev")
    yh, core = lax.div(g, 2), lax.rem(g, 2)
    x, yl, z = lax.div(me, 8), lax.rem(lax.div(me, 4), 2), lax.rem(me, 4)
    place = x * 4 + z
    other_half = (1 - yh) * 2

    sibling = (yh * 2 + 1 - core, me)
    a_side = (g, x * 8 + (1 - yl) * 4 + z)
    b_side = (other_half + core, x * 8 + (1 - yl) * 4 + z)
    b_cross = (other_half + 1 - core, x * 8 + (1 - yl) * 4 + z)
    d_side = (other_half + core, me)

    def plane_peer(i):
        px = lax.rem(x + lax.div(i, 4), 4)
        pz = lax.rem(z + lax.rem(i, 4), 4)
        return px, pz

    def columns(k):
        return pl.ds(pl.multiple_of(k * width, width), width)

    def remote(src, dst, send, recv, target):
        pltpu.make_async_remote_copy(
            src_ref=src, dst_ref=dst, send_sem=send, recv_sem=recv,
            device_id=target, device_id_type=MESH,
        ).start()

    rows16 = pl.ds(pl.multiple_of(place * 16, 16), 16)
    pltpu.make_async_copy(light.at[yh, core, rows16], lbuf.at[0], light_recv).start()
    for k in range(CHUNKS):
        pltpu.make_async_copy(
            grad.at[:, :, core, :, columns(k)], pbuf.at[k], load_sem.at[k]
        ).start()
    for k in range(CHUNKS):
        pltpu.make_async_copy(field.at[:, :, columns(k)], obuf.at[k], field_sem.at[k]).start()

    barrier = pltpu.get_barrier_semaphore()
    for target in (sibling, b_side, b_cross, d_side):
        pl.semaphore_signal(barrier, 1, device_id=target, device_id_type=MESH)

    def greet(i, carry):
        pl.semaphore_signal(
            barrier, 1, device_id=(g, lax.rem(me + i, 32)), device_id_type=MESH
        )
        return carry

    lax.fori_loop(1, 32, greet, 0)
    pl.semaphore_wait(barrier, 35)

    remote(light.at[yh, 1 - core, rows16], lbuf.at[1], light_send, light_recv, sibling)
    remote(light.at[1 - yh, core, rows16], lbuf.at[2], light_send, light_recv, b_side)
    remote(light.at[1 - yh, 1 - core, rows16], lbuf.at[3], light_send, light_recv, b_cross)

    for k in range(CHUNKS):
        remote(
            grad.at[:, :, 1 - core, :, columns(k)], cbuf.at[k],
            core_send, core_recv.at[k], sibling,
        )

    wait_for(lbuf, light_recv)

    for k in range(CHUNKS):
        cols = pl.ds(k * width, width)
        dbuf[k, rows16, :] = (
            lbuf[0, :, cols] + lbuf[1, :, cols] + lbuf[2, :, cols] + lbuf[3, :, cols] + damping
        )

    def spread(n, carry):
        k, i = lax.div(n, 15), lax.rem(n, 15) + 1
        px, pz = plane_peer(i)
        remote(
            dbuf.at[k, rows16], dbuf.at[k, rows16], damp_send, damp_recv.at[k],
            (g, px * 8 + yl * 4 + pz),
        )
        return carry

    lax.fori_loop(0, 15 * CHUNKS, spread, 0)

    mine = pl.ds(pl.multiple_of(yl * 128, 128), 128)
    theirs = pl.ds(pl.multiple_of((1 - yl) * 128, 128), 128)

    def chip_sum(k, carry):
        wait_for(pbuf.at[k], load_sem.at[k])
        wait_for(cbuf.at[k], core_recv.at[k])
        pbuf[k] = pbuf[k] + cbuf[k]
        remote(pbuf.at[k, :, 1 - yh, mine], from_d.at[k], y_send.at[0], y_recv.at[0, k], d_side)
        remote(pbuf.at[k, :, 1 - yh, theirs], from_b.at[k], y_send.at[1], y_recv.at[1, k], b_side)
        return carry

    lax.fori_loop(0, CHUNKS, chip_sum, 0)

    def send_near(k, carry):
        wait_for(obuf.at[k], field_sem.at[k])
        wait_for(dbuf.at[k, pl.ds(0, 240)], damp_recv.at[k])
        damp = dbuf[k, theirs, :]
        pbuf[k, :, yh, theirs] = obuf[k, :, theirs, :] * damp[None] - pbuf[k, :, yh, theirs]
        remote(pbuf.at[k, :, yh, theirs], from_a.at[k], y_send.at[2], y_recv.at[2, k], a_side)
        return carry

    lax.fori_loop(0, CHUNKS, send_near, 0)

    def send_plane(k):
        wait_for(from_d.at[k], y_recv.at[0, k])
        damp = dbuf[k, mine, :]
        sbuf[k, :, yl] = obuf[k, :, mine, :] * damp[None] - pbuf[k, :, yh, mine] - from_d[k]
        wait_for(from_b.at[k], y_recv.at[1, k])
        wait_for(from_a.at[k], y_recv.at[2, k])
        sbuf[k, :, 1 - yl] = from_a[k] - from_b[k]

        def send(i, carry):
            px, pz = plane_peer(i)
            rows = pl.ds(pl.multiple_of((px * 4 + pz) * 8, 8), 8)
            remote(
                sbuf.at[k, :, :, rows], xbuf.at[k, :, x, :, z], plane_send, plane_recv.at[k],
                (g, px * 8 + yl * 4 + pz),
            )
            return carry

        lax.fori_loop(1, 16, send, 0)
        own = pl.ds(pl.multiple_of(place * 8, 8), 8)
        pltpu.make_async_copy(
            sbuf.at[k, :, :, own], xbuf.at[k, :, x, :, z], plane_recv.at[k]
        ).start()

    own_rows = pl.ds(pl.multiple_of(yl * 128 + place * 8, 8), 8)

    def mix_and_return(k):
        wait_for(xbuf.at[k], plane_recv.at[k])
        inverse = 1.0 / dbuf[k, own_rows, :]
        for part in range(2):
            block = xbuf[k, part].reshape(256, width)
            mixed = jnp.dot(
                mix_ref[...], block, precision=lax.Precision.HIGHEST,
                preferred_element_type=jnp.float32,
            )
            ybuf[k, part] = mixed.reshape(32, 8, width) * inverse[None]

        def send(i, carry):
            target = lax.rem(me + i, 32)
            remote(
                ybuf.at[k, :, target], out.at[:, own_rows, columns(k)], back_send, back_recv,
                (g, target),
            )
            return carry

        lax.fori_loop(1, 32, send, 0)
        pltpu.make_async_copy(
            ybuf.at[k, :, me], out.at[:, own_rows, columns(k)], back_recv
        ).start()

    send_plane(0)

    def steady(k, carry):
        send_plane(k)
        mix_and_return(k - 1)
        return carry

    lax.fori_loop(1, CHUNKS, steady, 0)
    mix_and_return(CHUNKS - 1)

    wait_for(lbuf.at[pl.ds(0, 3)], light_send)
    wait_for(cbuf, core_send)
    wait_for(dbuf.at[:, pl.ds(0, 240)], damp_send)
    wait_for(from_d, y_send.at[0])
    wait_for(from_b, y_send.at[1])
    wait_for(from_a, y_send.at[2])
    wait_for(sbuf.at[:, :, :, pl.ds(0, 120)], plane_send)
    wait_for(ybuf.at[:, :, pl.ds(0, 31)], back_send)
    wait_for(out, back_recv)


def per_device(grad_parts, light_parts, object_field):
    rows, columns = light_parts.shape[1:]
    slices = 32
    quarter = rows // 4
    width = columns // CHUNKS
    f32 = jnp.float32
    grad = grad_parts.reshape(2, 2, 2, quarter, columns)
    light = light_parts.reshape(2, 2, quarter, columns)
    field = object_field.reshape(2, quarter, columns)
    any_space = pl.BlockSpec(memory_space=pl.ANY)
    dma = pltpu.SemaphoreType.DMA
    half = quarter // 2
    mixed = pl.pallas_call(
        kernel,
        out_shape=jax.ShapeDtypeStruct((2, quarter, columns), f32),
        in_specs=[pl.BlockSpec(memory_space=pltpu.VMEM), any_space, any_space, any_space],
        out_specs=any_space,
        scratch_shapes=[
            pltpu.VMEM((CHUNKS, 2, 2, quarter, width), f32),
            pltpu.VMEM((CHUNKS, 2, 2, quarter, width), f32),
            pltpu.VMEM((CHUNKS, 2, quarter, width), f32),
            pltpu.VMEM((4, 16, columns), f32),
            pltpu.VMEM((CHUNKS, quarter, width), f32),
            pltpu.VMEM((CHUNKS, 2, half, width), f32),
            pltpu.VMEM((CHUNKS, 2, half, width), f32),
            pltpu.VMEM((CHUNKS, 2, half, width), f32),
            pltpu.VMEM((CHUNKS, 2, 2, half, width), f32),
            pltpu.VMEM((CHUNKS, 2, 4, 2, 4, 8, width), f32),
            pltpu.VMEM((CHUNKS, 2, slices, 8, width), f32),
            dma((CHUNKS,)), dma((CHUNKS,)),
            dma, dma((CHUNKS,)),
            dma, dma,
            dma, dma((CHUNKS,)),
            dma((3,)), dma((3, CHUNKS)),
            dma, dma((CHUNKS,)),
            dma, dma,
        ],
        compiler_params=pltpu.CompilerParams(
            collective_id=0, has_side_effects=True, vmem_limit_bytes=48 * 2**20
        ),
    )(jnp.asarray(mixing_matrix(slices, 8)), grad, light, field)
    amplitude = jnp.sqrt(mixed[0] * mixed[0] + mixed[1] * mixed[1])
    factor = ceiling / jnp.maximum(amplitude, ceiling)
    return (mixed * factor[None]).reshape(object_field.shape)


def solution(mesh):
    in_specs = (
        P("grp", None, "dev", None, None),
        P("grp", None, None),
        P(None, "dev", "grp", None),
    )
    out_specs = P(None, "dev", "grp", None)
    return jax.shard_map(
        per_device, mesh=mesh, in_specs=in_specs, out_specs=out_specs, check_vma=False
    )
```

```python
import functools
import math

import jax
import jax.numpy as jnp
import numpy as np
from jax import lax
from jax.experimental import pallas as pl
from jax.experimental.pallas import tpu as pltpu
from jax.sharding import PartitionSpec as P

damping = 0.05
ceiling = 0.4
MESH = pl.DeviceIdType.MESH
CHUNKS = 4
PLAN = (
    ("sum", 0),
    ("ed", 0),
    ("eb", 0),
    ("dr", 0),
    ("sum", 1),
    ("ed", 1),
    ("damp", 0),
    ("sum", 2),
    ("sum", 3),
    ("wd", 0),
    ("wf", 0),
    ("ea", 0),
    ("eb", 1),
    ("wd", 1),
    ("wf", 1),
    ("ea", 1),
    ("wf", 2),
    ("wf", 3),
    ("ed", 2),
    ("eb", 2),
    ("ea", 2),
    ("ed", 3),
    ("eb", 3),
    ("ea", 3),
    ("wm", 0),
    ("ep", 0),
    ("ep", 1),
    ("em", 0),
    ("er", 0),
    ("ep", 2),
    ("em", 1),
    ("er", 1),
    ("ep", 3),
    ("hop", 0),
    ("em", 2),
    ("er", 2),
    ("hop", 1),
    ("em", 3),
    ("er", 3),
    ("hop", 2),
    ("hop", 3),
)


def mixing_matrix(count, lanes):
    wavenumber = np.arange(count)
    signed = np.where(2 * wavenumber < count, wavenumber, wavenumber - count)
    taper = np.exp(-((signed / (count / 8.0)) ** 2))
    offsets = (wavenumber[:, None] - wavenumber[None, :]) % count
    angles = 2.0 * math.pi / count * ((wavenumber[None, None, :] * offsets[:, :, None]) % count)
    mixing = np.sum(taper * np.cos(angles), axis=2) / count
    rows = mixing.reshape(4, 2, 4, count).transpose(1, 0, 2, 3).reshape(2, 16, count)
    return np.stack([np.kron(half, np.eye(lanes)) for half in rows]).astype(np.float32)


def wait_for(ref, sem):
    pltpu.make_async_copy(ref, ref, sem).wait()


def kernel(
    mix_hbm, grad, light, field, out,
    mix_ref, pbuf, cbuf, obuf, lbuf, dbuf, from_a, from_b, from_d, sbuf, xbuf, ybuf, rbuf,
    mix_sem, load_sem, field_sem, core_send, core_recv, light_send, light_recv,
    damp_send, damp_recv, y_send, y_recv, plane_send, plane_recv, back_send, back_recv,
    hop_send, hop_recv,
):
    width = pbuf.shape[-1]
    g = lax.axis_index("grp")
    me = lax.axis_index("dev")
    yh, core = lax.div(g, 2), lax.rem(g, 2)
    x, yl, z = lax.div(me, 8), lax.rem(lax.div(me, 4), 2), lax.rem(me, 4)
    place = x * 4 + z
    other_half = (1 - yh) * 2
    across = x * 8 + (1 - yl) * 4 + z

    sibling = (yh * 2 + 1 - core, me)
    a_side = (g, across)
    b_side = (other_half + core, across)
    b_cross = (other_half + 1 - core, across)
    d_side = (other_half + core, me)

    def plane_peer(i):
        return lax.rem(x + lax.rem(i, 4), 4), lax.rem(z + i + lax.div(i, 4), 4)

    def columns(k):
        return pl.ds(k * width, width)

    def remote(src, dst, send, recv, target):
        pltpu.make_async_remote_copy(
            src_ref=src, dst_ref=dst, send_sem=send, recv_sem=recv,
            device_id=target, device_id_type=MESH,
        ).start()

    order = list(range(CHUNKS))

    rows16 = pl.ds(pl.multiple_of(place * 16, 16), 16)
    pltpu.make_async_copy(light.at[yh, core, rows16], lbuf.at[0], light_recv).start()
    for k in order:
        pltpu.make_async_copy(
            grad.at[:, :, core, :, columns(k)], pbuf.at[k], load_sem.at[k]
        ).start()
    for k in order:
        pltpu.make_async_copy(field.at[:, :, columns(k)], obuf.at[k], field_sem.at[k]).start()
    pltpu.make_async_copy(mix_hbm, mix_ref, mix_sem).start()

    barrier = pltpu.get_barrier_semaphore()
    for target in (sibling, a_side, b_side, b_cross, d_side):
        pl.semaphore_signal(barrier, 1, device_id=target, device_id_type=MESH)

    def greet(i, carry):
        px, pz = plane_peer(i)
        pl.semaphore_signal(
            barrier, 1, device_id=(g, px * 8 + yl * 4 + pz), device_id_type=MESH
        )
        return carry

    lax.fori_loop(1, 16, greet, 0)
    pl.semaphore_wait(barrier, 20)

    remote(light.at[yh, 1 - core, rows16], lbuf.at[1], light_send, light_recv, sibling)
    remote(light.at[1 - yh, core, rows16], lbuf.at[2], light_send, light_recv, b_side)
    remote(light.at[1 - yh, 1 - core, rows16], lbuf.at[3], light_send, light_recv, b_cross)

    for k in order:
        remote(
            grad.at[:, :, 1 - core, :, columns(k)], cbuf.at[k],
            core_send, core_recv.at[k], sibling,
        )

    mine = pl.ds(pl.multiple_of(yl * 128, 128), 128)
    theirs = pl.ds(pl.multiple_of((1 - yl) * 128, 128), 128)

    def damp_of(k, which):
        wide = dbuf.shape[-1]
        half, start = k * width // wide, k * width % wide
        cols = slice(start, start + width)
        if which == "all":
            return dbuf[half, :, :, :, cols].reshape(256, width)
        if which == "mine":
            return dbuf[half, pl.ds(yl * 2, 2), :, :, cols].reshape(128, width)
        if which == "theirs":
            return dbuf[half, pl.ds((1 - yl) * 2, 2), :, :, cols].reshape(128, width)
        row = yl * 128 + place * 8
        return dbuf[half, lax.div(row, 64), lax.rem(lax.div(row, 16), 4),
                    pl.ds(pl.multiple_of(lax.rem(row, 16), 8), 8), cols]

    def chip_sum(k):
        wait_for(pbuf.at[k], load_sem.at[k])
        wait_for(cbuf.at[k], core_recv.at[k])
        pbuf[k] = pbuf[k] + cbuf[k]

    def early_d_send(k):
        remote(pbuf.at[k, :, 1 - yh, mine], from_d.at[k], y_send.at[0], y_recv.at[0, k], d_side)

    def early_b_send(k):
        remote(pbuf.at[k, :, 1 - yh, theirs], from_b.at[k], y_send.at[1], y_recv.at[1, k], b_side)

    def early_a_send(k):
        damp = damp_of(k, 'theirs')
        pbuf[k, :, yh, theirs] = obuf[k, :, theirs, :] * damp[None] - pbuf[k, :, yh, theirs]
        remote(pbuf.at[k, :, yh, theirs], from_a.at[k], y_send.at[2], y_recv.at[2, k], a_side)

    def ring(coordinate, i):
        return lax.rem(coordinate + i, 4)

    def reduce_damp():
        wait_for(lbuf, light_recv)
        total = lbuf[0] + lbuf[1] + lbuf[2] + lbuf[3] + damping
        wide = dbuf.shape[-1]
        for half in range(2):
            dbuf[half, x, z] = total[:, half * wide:(half + 1) * wide]
        for i in range(1, 4):
            remote(
                dbuf.at[0, x, z], dbuf.at[0, x, z], damp_send.at[0], damp_recv.at[0],
                (g, x * 8 + yl * 4 + ring(z, i)),
            )
            remote(
                dbuf.at[1, x, z], dbuf.at[1, x, z], damp_send.at[1], damp_recv.at[1],
                (g, ring(x, i) * 8 + yl * 4 + z),
            )

    def spread_damp():
        wait_for(dbuf.at[0, 0, pl.ds(0, 3)], damp_recv.at[0])
        for i in range(1, 4):
            remote(
                dbuf.at[0, x], dbuf.at[0, x], damp_send.at[2], damp_recv.at[2],
                (g, ring(x, i) * 8 + yl * 4 + z),
            )
        wait_for(dbuf.at[1, 0, pl.ds(0, 3)], damp_recv.at[1])
        for i in range(1, 4):
            remote(
                dbuf.at[1, :, z], dbuf.at[1, :, z], damp_send.at[3], damp_recv.at[3],
                (g, x * 8 + yl * 4 + ring(z, i)),
            )

    def wait_damp(half):
        wait_for(dbuf.at[half, pl.ds(0, 3)], damp_recv.at[2 + half])

    def mix(half, block):
        return jnp.dot(
            mix_ref[half], block, precision=lax.Precision.HIGHEST,
            preferred_element_type=jnp.float32,
        ).reshape(16, 8, width)

    def early_plane(k):
        damp = damp_of(k, 'mine')
        wait_for(from_d.at[k], y_recv.at[0, k])
        sbuf[k, :, yl] = obuf[k, :, mine, :] * damp[None] - pbuf[k, :, yh, mine] - from_d[k]
        wait_for(from_b.at[k], y_recv.at[1, k])
        wait_for(from_a.at[k], y_recv.at[2, k])
        sbuf[k, :, 1 - yl] = from_a[k] - from_b[k]

        def send(i, carry):
            px, pz = plane_peer(i)
            rows = pl.ds(pl.multiple_of((px * 4 + pz) * 8, 8), 8)
            remote(
                sbuf.at[k, :, :, rows], xbuf.at[k, :, x, :, z], plane_send, plane_recv.at[k],
                (g, px * 8 + yl * 4 + pz),
            )
            return carry

        lax.fori_loop(1, 16, send, 0)
        own = pl.ds(pl.multiple_of(place * 8, 8), 8)
        pltpu.make_async_copy(
            sbuf.at[k, :, :, own], xbuf.at[k, :, x, :, z], plane_recv.at[k]
        ).start()

    def early_mix(k):
        wait_for(xbuf.at[k], plane_recv.at[k])
        inverse = 1.0 / damp_of(k, 'early')
        for half in range(2):
            real, imag = (
                mix(half, xbuf[k, part].reshape(256, width)) * inverse[None] for part in range(2)
            )
            amplitude = jnp.sqrt(real * real + imag * imag)
            factor = ceiling / jnp.maximum(amplitude, ceiling)
            real, imag = real * factor, imag * factor
            ybuf[k, 0, half] = real
            ybuf[k, 1, half] = imag

    def early_return(k):
        rows = pl.ds(pl.multiple_of(place * 8, 8), 8)

        def send(i, carry):
            px, pz = plane_peer(i)
            remote(
                ybuf.at[k, :, :, px * 4 + pz], rbuf.at[k, :, :, rows], back_send, back_recv.at[k],
                (g, px * 8 + yl * 4 + pz),
            )
            return carry

        lax.fori_loop(1, 16, send, 0)
        pltpu.make_async_copy(
            ybuf.at[k, :, :, place], rbuf.at[k, :, :, rows], back_recv.at[k]
        ).start()

    def hop(k):
        wait_for(rbuf.at[k], back_recv.at[k])
        remote(
            rbuf.at[k, :, 1 - yl], out.at[:, mine, columns(k)], hop_send, hop_recv, a_side
        )
        pltpu.make_async_copy(
            rbuf.at[k, :, yl], out.at[:, mine, columns(k)], hop_recv
        ).start()

    steps = {
        "sum": chip_sum, "ed": early_d_send, "eb": early_b_send, "ea": early_a_send,
        "dr": lambda k: reduce_damp(), "damp": lambda k: spread_damp(), "wd": wait_damp,
        "ep": early_plane, "em": early_mix, "er": early_return, "hop": hop,
        "wm": lambda k: wait_for(mix_ref, mix_sem),
        "wf": lambda k: wait_for(obuf.at[k], field_sem.at[k]),
    }
    for name, k in PLAN:
        steps[name](k)

    wait_for(lbuf.at[pl.ds(0, 3)], light_send)
    wait_for(cbuf, core_send)
    wait_for(dbuf.at[0, 0, pl.ds(0, 3)], damp_send.at[0])
    wait_for(dbuf.at[0, 0, pl.ds(0, 3)], damp_send.at[1])
    wait_for(dbuf.at[0, pl.ds(0, 3)], damp_send.at[2])
    wait_for(dbuf.at[0, pl.ds(0, 3)], damp_send.at[3])
    wait_for(from_d, y_send.at[0])
    wait_for(from_b, y_send.at[1])
    wait_for(from_a, y_send.at[2])
    wait_for(sbuf.at[:, :, :, pl.ds(0, 120)], plane_send)
    wait_for(rbuf.at[:, :, :, pl.ds(0, 120)], back_send)
    wait_for(rbuf.at[:, :, 0], hop_send)
    wait_for(out, hop_recv)


def per_device(grad_parts, light_parts, object_field):
    rows, columns = light_parts.shape[1:]
    slices = 32
    quarter = rows // 4
    half = quarter // 2
    width = columns // CHUNKS
    f32 = jnp.float32
    grad = grad_parts.reshape(2, 2, 2, quarter, columns)
    light = light_parts.reshape(2, 2, quarter, columns)
    field = object_field.reshape(2, quarter, columns)
    matrix = jnp.asarray(mixing_matrix(slices, 8))
    in_hbm = pl.BlockSpec(memory_space=pltpu.HBM)
    in_vmem = pl.BlockSpec(memory_space=pltpu.VMEM)
    dma = pltpu.SemaphoreType.DMA
    updated = pl.pallas_call(
        kernel,
        out_shape=jax.ShapeDtypeStruct((2, quarter, columns), f32),
        in_specs=[in_hbm] * 4,
        out_specs=in_vmem,
        scratch_shapes=[
            pltpu.VMEM(matrix.shape, f32),
            pltpu.VMEM((CHUNKS, 2, 2, quarter, width), f32),
            pltpu.VMEM((CHUNKS, 2, 2, quarter, width), f32),
            pltpu.VMEM((CHUNKS, 2, quarter, width), f32),
            pltpu.VMEM((4, 16, columns), f32),
            pltpu.VMEM((2, 4, 4, quarter // 16, columns // 2), f32),
            pltpu.VMEM((CHUNKS, 2, half, width), f32),
            pltpu.VMEM((CHUNKS, 2, half, width), f32),
            pltpu.VMEM((CHUNKS, 2, half, width), f32),
            pltpu.VMEM((CHUNKS, 2, 2, half, width), f32),
            pltpu.VMEM((CHUNKS, 2, 4, 2, 4, 8, width), f32),
            pltpu.VMEM((CHUNKS, 2, 2, slices // 2, 8, width), f32),
            pltpu.VMEM((CHUNKS, 2, 2, half, width), f32),
            dma, dma((CHUNKS,)), dma((CHUNKS,)),
            dma, dma((CHUNKS,)),
            dma, dma,
            dma((4,)), dma((4,)),
            dma((3,)), dma((3, CHUNKS)),
            dma, dma((CHUNKS,)),
            dma, dma((CHUNKS,)),
            dma, dma,
        ],
        compiler_params=pltpu.CompilerParams(
            collective_id=0, has_side_effects=True, vmem_limit_bytes=48 * 2**20
        ),
    )(matrix, grad, light, field)
    return updated.reshape(object_field.shape)


def solution(mesh):
    in_specs = (
        P("grp", None, "dev", None, None),
        P("grp", None, None),
        P(None, "dev", "grp", None),
    )
    out_specs = P(None, "dev", "grp", None)
    return jax.shard_map(
        per_device, mesh=mesh, in_specs=in_specs, out_specs=out_specs, check_vma=False
    )
```

```python
import functools
import math

import jax
import jax.numpy as jnp
import numpy as np
from jax import lax
from jax.experimental import pallas as pl
from jax.experimental.pallas import tpu as pltpu
from jax.sharding import PartitionSpec as P

damping = 0.05
ceiling = 0.4
MESH = pl.DeviceIdType.MESH
WIDTHS = (256, 256, 256, 128, 128)
CHUNKS = len(WIDTHS)
PLAN = (
    ("sum", 0),
    ("ed", 0),
    ("eb", 0),
    ("dr", 0),
    ("sum", 1),
    ("ed", 1),
    ("damp", 0),
    ("sum", 2),
    ("sum", 3),
    ("sum", 4),
    ("wd", 0),
    ("wf", 0),
    ("ea", 0),
    ("eb", 1),
    ("wd", 1),
    ("wf", 1),
    ("wf", 2),
    ("wf", 3),
    ("wf", 4),
    ("ea", 1),
    ("ed", 2),
    ("eb", 2),
    ("ea", 2),
    ("ed", 3),
    ("eb", 3),
    ("ea", 3),
    ("ed", 4),
    ("eb", 4),
    ("ea", 4),
    ("ep", 0),
    ("ep", 1),
    ("em", 0),
    ("er", 0),
    ("ep", 2),
    ("em", 1),
    ("er", 1),
    ("ep", 3),
    ("em", 2),
    ("er", 2),
    ("ep", 4),
    ("hop", 0),
    ("hop", 1),
    ("em", 3),
    ("er", 3),
    ("hop", 2),
    ("em", 4),
    ("er", 4),
    ("hop", 3),
    ("hop", 4),
)


def mixing_row(count):
    wavenumber = np.arange(count)
    signed = np.where(2 * wavenumber < count, wavenumber, wavenumber - count)
    taper = np.exp(-((signed / (count / 8.0)) ** 2))
    angles = 2.0 * math.pi / count * (wavenumber[None, :] * wavenumber[:, None] % count)
    return [float(value) for value in np.sum(taper * np.cos(angles), axis=1) / count]


def mixing_matrix(half):
    shape = (128, 256)
    row, column = (lax.broadcasted_iota(jnp.int32, shape, axis) for axis in range(2))
    out = (row // 32) * 8 + half * 4 + (row // 8) % 4
    apart = jnp.abs(out - column // 8)
    apart = jnp.where(row % 8 == column % 8, jnp.minimum(apart, 32 - apart), -1)
    values = mixing_row(32)
    matrix = jnp.zeros(shape, jnp.float32)
    for distance in range(17):
        matrix = jnp.where(apart == distance, values[distance], matrix)
    return matrix


def wait_for(ref, sem):
    pltpu.make_async_copy(ref, ref, sem).wait()


def kernel(
    grad, light, field, out,
    mix_ref, pbuf, cbuf, obuf, lbuf, dbuf, from_a, from_b, from_d, sbuf, xbuf, ybuf, rbuf,
    load_sem, field_sem, core_send, core_recv, light_send, light_recv,
    damp_send, damp_recv, y_send, y_recv, plane_send, plane_recv, back_send, back_recv,
    hop_send, hop_recv,
):
    g = lax.axis_index("grp")
    me = lax.axis_index("dev")
    yh, core = lax.div(g, 2), lax.rem(g, 2)
    x, yl, z = lax.div(me, 8), lax.rem(lax.div(me, 4), 2), lax.rem(me, 4)
    place = x * 4 + z
    other_half = (1 - yh) * 2
    across = x * 8 + (1 - yl) * 4 + z

    sibling = (yh * 2 + 1 - core, me)
    a_side = (g, across)
    b_side = (other_half + core, across)
    b_cross = (other_half + 1 - core, across)
    d_side = (other_half + core, me)

    def plane_peer(i):
        return lax.rem(x + lax.rem(i, 4), 4), lax.rem(z + i + lax.div(i, 4), 4)

    def columns(k):
        return pl.ds(sum(WIDTHS[:k]), WIDTHS[k])

    def remote(src, dst, send, recv, target):
        pltpu.make_async_remote_copy(
            src_ref=src, dst_ref=dst, send_sem=send, recv_sem=recv,
            device_id=target, device_id_type=MESH,
        ).start()

    order = list(range(CHUNKS))

    rows16 = pl.ds(pl.multiple_of(place * 16, 16), 16)
    pltpu.make_async_copy(light.at[yh, core, rows16], lbuf.at[0], light_recv).start()
    for k in order:
        pltpu.make_async_copy(
            grad.at[:, :, core, :, columns(k)], pbuf[k], load_sem.at[k]
        ).start()
    for k in order:
        pltpu.make_async_copy(field.at[:, :, columns(k)], obuf[k], field_sem.at[k]).start()

    barrier = pltpu.get_barrier_semaphore()
    for target in (sibling, a_side, b_side, b_cross, d_side):
        pl.semaphore_signal(barrier, 1, device_id=target, device_id_type=MESH)

    def greet(i, carry):
        px, pz = plane_peer(i)
        pl.semaphore_signal(
            barrier, 1, device_id=(g, px * 8 + yl * 4 + pz), device_id_type=MESH
        )
        return carry

    lax.fori_loop(1, 16, greet, 0)
    for half in range(2):
        mix_ref[half] = mixing_matrix(half)
    pl.semaphore_wait(barrier, 20)

    remote(light.at[yh, 1 - core, rows16], lbuf.at[1], light_send, light_recv, sibling)
    remote(light.at[1 - yh, core, rows16], lbuf.at[2], light_send, light_recv, b_side)
    remote(light.at[1 - yh, 1 - core, rows16], lbuf.at[3], light_send, light_recv, b_cross)

    for k in order:
        remote(
            grad.at[:, :, 1 - core, :, columns(k)], cbuf[k],
            core_send.at[k], core_recv.at[k], sibling,
        )

    mine = pl.ds(pl.multiple_of(yl * 128, 128), 128)
    theirs = pl.ds(pl.multiple_of((1 - yl) * 128, 128), 128)

    def damp_of(k, which):
        wide = dbuf.shape[-1]
        width = WIDTHS[k]
        half, start = sum(WIDTHS[:k]) // wide, sum(WIDTHS[:k]) % wide
        cols = slice(start, start + width)
        if which == "all":
            return dbuf[half, :, :, :, cols].reshape(256, width)
        if which == "mine":
            return dbuf[half, pl.ds(yl * 2, 2), :, :, cols].reshape(128, width)
        if which == "theirs":
            return dbuf[half, pl.ds((1 - yl) * 2, 2), :, :, cols].reshape(128, width)
        row = yl * 128 + place * 8
        return dbuf[half, lax.div(row, 64), lax.rem(lax.div(row, 16), 4),
                    pl.ds(pl.multiple_of(lax.rem(row, 16), 8), 8), cols]

    def chip_sum(k):
        wait_for(pbuf[k], load_sem.at[k])
        wait_for(cbuf[k], core_recv.at[k])
        pbuf[k][...] = pbuf[k][...] + cbuf[k][...]

    def early_d_send(k):
        remote(pbuf[k].at[:, 1 - yh, mine], from_d[k], y_send.at[0, k], y_recv.at[0, k], d_side)

    def early_b_send(k):
        remote(pbuf[k].at[:, 1 - yh, theirs], from_b[k], y_send.at[1, k], y_recv.at[1, k], b_side)

    def early_a_send(k):
        damp = damp_of(k, 'theirs')
        pbuf[k][:, yh, theirs] = obuf[k][:, theirs, :] * damp[None] - pbuf[k][:, yh, theirs]
        remote(pbuf[k].at[:, yh, theirs], from_a[k], y_send.at[2, k], y_recv.at[2, k], a_side)

    def ring(coordinate, i):
        return lax.rem(coordinate + i, 4)

    def reduce_damp():
        wait_for(lbuf, light_recv)
        total = lbuf[0] + lbuf[1] + lbuf[2] + lbuf[3] + damping
        wide = dbuf.shape[-1]
        for half in range(2):
            dbuf[half, x, z] = total[:, half * wide:(half + 1) * wide]
        for i in range(1, 4):
            remote(
                dbuf.at[0, x, z], dbuf.at[0, x, z], damp_send.at[0], damp_recv.at[0],
                (g, x * 8 + yl * 4 + ring(z, i)),
            )
            remote(
                dbuf.at[1, x, z], dbuf.at[1, x, z], damp_send.at[1], damp_recv.at[1],
                (g, ring(x, i) * 8 + yl * 4 + z),
            )

    def spread_damp():
        wait_for(dbuf.at[0, 0, pl.ds(0, 3)], damp_recv.at[0])
        for i in range(1, 4):
            remote(
                dbuf.at[0, x], dbuf.at[0, x], damp_send.at[2], damp_recv.at[2],
                (g, ring(x, i) * 8 + yl * 4 + z),
            )
        wait_for(dbuf.at[1, 0, pl.ds(0, 3)], damp_recv.at[1])
        for i in range(1, 4):
            remote(
                dbuf.at[1, :, z], dbuf.at[1, :, z], damp_send.at[3], damp_recv.at[3],
                (g, x * 8 + yl * 4 + ring(z, i)),
            )

    def wait_damp(half):
        wait_for(dbuf.at[half, pl.ds(0, 3)], damp_recv.at[2 + half])

    def mix(half, block):
        return jnp.dot(
            mix_ref[half], block, precision=lax.Precision.HIGHEST,
            preferred_element_type=jnp.float32,
        ).reshape(16, 8, block.shape[1])

    def early_plane(k):
        damp = damp_of(k, 'mine')
        wait_for(from_d[k], y_recv.at[0, k])
        sbuf[k][:, yl] = obuf[k][:, mine, :] * damp[None] - pbuf[k][:, yh, mine] - from_d[k][...]
        wait_for(from_b[k], y_recv.at[1, k])
        wait_for(from_a[k], y_recv.at[2, k])
        sbuf[k][:, 1 - yl] = from_a[k][...] - from_b[k][...]

        def send(i, carry):
            px, pz = plane_peer(i)
            rows = pl.ds(pl.multiple_of((px * 4 + pz) * 8, 8), 8)
            remote(
                sbuf[k].at[:, :, rows], xbuf[k].at[:, x, :, z], plane_send.at[k], plane_recv.at[k],
                (g, px * 8 + yl * 4 + pz),
            )
            return carry

        lax.fori_loop(1, 16, send, 0)
        own = pl.ds(pl.multiple_of(place * 8, 8), 8)
        pltpu.make_async_copy(
            sbuf[k].at[:, :, own], xbuf[k].at[:, x, :, z], plane_recv.at[k]
        ).start()

    def early_mix(k):
        wait_for(xbuf[k], plane_recv.at[k])
        inverse = 1.0 / damp_of(k, 'early')
        for half in range(2):
            real, imag = (
                mix(half, xbuf[k][part].reshape(256, WIDTHS[k])) * inverse[None] for part in range(2)
            )
            amplitude = jnp.sqrt(real * real + imag * imag)
            factor = ceiling / jnp.maximum(amplitude, ceiling)
            real, imag = real * factor, imag * factor
            ybuf[k][0, half] = real
            ybuf[k][1, half] = imag

    def early_return(k):
        rows = pl.ds(pl.multiple_of(place * 8, 8), 8)

        def send(i, carry):
            px, pz = plane_peer(i)
            remote(
                ybuf[k].at[:, :, px * 4 + pz], rbuf[k].at[:, :, rows], back_send.at[k], back_recv.at[k],
                (g, px * 8 + yl * 4 + pz),
            )
            return carry

        lax.fori_loop(1, 16, send, 0)
        pltpu.make_async_copy(
            ybuf[k].at[:, :, place], rbuf[k].at[:, :, rows], back_recv.at[k]
        ).start()

    def hop(k):
        wait_for(rbuf[k], back_recv.at[k])
        remote(
            rbuf[k].at[:, 1 - yl], out.at[:, mine, columns(k)], hop_send.at[k], hop_recv.at[k], a_side
        )
        pltpu.make_async_copy(
            rbuf[k].at[:, yl], out.at[:, mine, columns(k)], hop_recv.at[k]
        ).start()

    steps = {
        "sum": chip_sum, "ed": early_d_send, "eb": early_b_send, "ea": early_a_send,
        "dr": lambda k: reduce_damp(), "damp": lambda k: spread_damp(), "wd": wait_damp,
        "ep": early_plane, "em": early_mix, "er": early_return, "hop": hop,
        "wf": lambda k: wait_for(obuf[k], field_sem.at[k]),
    }
    for name, k in PLAN:
        steps[name](k)

    wait_for(lbuf.at[pl.ds(0, 3)], light_send)
    wait_for(dbuf.at[0, 0, pl.ds(0, 3)], damp_send.at[0])
    wait_for(dbuf.at[0, 0, pl.ds(0, 3)], damp_send.at[1])
    wait_for(dbuf.at[0, pl.ds(0, 3)], damp_send.at[2])
    wait_for(dbuf.at[0, pl.ds(0, 3)], damp_send.at[3])
    for k in range(CHUNKS):
        wait_for(cbuf[k], core_send.at[k])
        wait_for(from_d[k], y_send.at[0, k])
        wait_for(from_b[k], y_send.at[1, k])
        wait_for(from_a[k], y_send.at[2, k])
        wait_for(sbuf[k].at[:, :, pl.ds(0, 120)], plane_send.at[k])
        wait_for(rbuf[k].at[:, :, pl.ds(0, 120)], back_send.at[k])
        wait_for(rbuf[k].at[:, 0], hop_send.at[k])
        wait_for(out.at[:, :, columns(k)], hop_recv.at[k])


def per_device(grad_parts, light_parts, object_field):
    rows, columns = light_parts.shape[1:]
    slices = 32
    quarter = rows // 4
    half = quarter // 2
    f32 = jnp.float32
    grad = grad_parts.reshape(2, 2, 2, quarter, columns)
    light = light_parts.reshape(2, 2, quarter, columns)
    field = object_field.reshape(2, quarter, columns)
    in_hbm = pl.BlockSpec(memory_space=pltpu.HBM)
    in_vmem = pl.BlockSpec(memory_space=pltpu.VMEM)
    dma = pltpu.SemaphoreType.DMA

    def per_chunk(*shape):
        return tuple(pltpu.VMEM((*shape, width), f32) for width in WIDTHS)

    updated = pl.pallas_call(
        kernel,
        out_shape=jax.ShapeDtypeStruct((2, quarter, columns), f32),
        in_specs=[in_hbm] * 3,
        out_specs=in_vmem,
        scratch_shapes=[
            pltpu.VMEM((2, 128, 256), f32),
            per_chunk(2, 2, quarter),
            per_chunk(2, 2, quarter),
            per_chunk(2, quarter),
            pltpu.VMEM((4, 16, columns), f32),
            pltpu.VMEM((2, 4, 4, quarter // 16, columns // 2), f32),
            per_chunk(2, half),
            per_chunk(2, half),
            per_chunk(2, half),
            per_chunk(2, 2, half),
            per_chunk(2, 4, 2, 4, 8),
            per_chunk(2, 2, slices // 2, 8),
            per_chunk(2, 2, half),
            dma((CHUNKS,)), dma((CHUNKS,)),
            dma((CHUNKS,)), dma((CHUNKS,)),
            dma, dma,
            dma((4,)), dma((4,)),
            dma((3, CHUNKS)), dma((3, CHUNKS)),
            dma((CHUNKS,)), dma((CHUNKS,)),
            dma((CHUNKS,)), dma((CHUNKS,)),
            dma((CHUNKS,)), dma((CHUNKS,)),
        ],
        compiler_params=pltpu.CompilerParams(
            collective_id=0, has_side_effects=True, vmem_limit_bytes=51 * 2**20
        ),
    )(grad, light, field)
    return updated.reshape(object_field.shape)


def solution(mesh):
    in_specs = (
        P("grp", None, "dev", None, None),
        P("grp", None, None),
        P(None, "dev", "grp", None),
    )
    out_specs = P(None, "dev", "grp", None)
    return jax.shard_map(
        per_device, mesh=mesh, in_specs=in_specs, out_specs=out_specs, check_vma=False
    )
```

```python
import functools
import math

import jax
import jax.numpy as jnp
import numpy as np
from jax import lax
from jax.experimental import pallas as pl
from jax.experimental.pallas import tpu as pltpu
from jax.sharding import PartitionSpec as P

damping = 0.05
ceiling = 0.4
MESH = pl.DeviceIdType.MESH
WIDTHS = (256, 256, 256, 128, 128)
CHUNKS = len(WIDTHS)
PLAN = (
    ("sum", 0),
    ("ed", 0),
    ("eb", 0),
    ("dr", 0),
    ("sum", 1),
    ("ed", 1),
    ("damp", 0),
    ("sum", 2),
    ("sum", 3),
    ("sum", 4),
    ("wd", 0),
    ("wf", 0),
    ("ea", 0),
    ("eb", 1),
    ("wd", 1),
    ("wf", 1),
    ("wf", 2),
    ("wf", 3),
    ("wf", 4),
    ("ea", 1),
    ("ed", 2),
    ("eb", 2),
    ("ea", 2),
    ("ed", 3),
    ("ed", 4),
    ("eb", 3),
    ("eb", 4),
    ("ea", 3),
    ("ea", 4),
    ("ep", 0),
    ("ep", 1),
    ("em", 0),
    ("er", 0),
    ("ep", 2),
    ("em", 1),
    ("er", 1),
    ("ep", 3),
    ("em", 2),
    ("er", 2),
    ("ep", 4),
    ("hop", 0),
    ("hop", 1),
    ("em", 3),
    ("er", 3),
    ("hop", 2),
    ("em", 4),
    ("er", 4),
    ("hop", 3),
    ("hop", 4),
)


def mixing_row(count):
    wavenumber = np.arange(count)
    signed = np.where(2 * wavenumber < count, wavenumber, wavenumber - count)
    taper = np.exp(-((signed / (count / 8.0)) ** 2))
    angles = 2.0 * math.pi / count * (wavenumber[None, :] * wavenumber[:, None] % count)
    return [float(value) for value in np.sum(taper * np.cos(angles), axis=1) / count]


def mixing_matrix(half):
    shape = (128, 256)
    row, column = (lax.broadcasted_iota(jnp.int32, shape, axis) for axis in range(2))
    out = (row // 32) * 8 + half * 4 + (row // 8) % 4
    apart = jnp.abs(out - column // 8)
    apart = jnp.where(row % 8 == column % 8, jnp.minimum(apart, 32 - apart), -1)
    values = mixing_row(32)
    matrix = jnp.zeros(shape, jnp.float32)
    for distance in range(17):
        matrix = jnp.where(apart == distance, values[distance], matrix)
    return matrix


def wait_for(ref, sem):
    pltpu.make_async_copy(ref, ref, sem).wait()


def kernel(
    grad, light, field, out,
    mix_ref, pbuf, cbuf, obuf, lbuf, dbuf, from_a, from_b, from_d, sbuf, xbuf, ybuf, rbuf,
    load_sem, field_sem, core_send, core_recv, light_send, light_recv,
    damp_send, damp_recv, y_send, y_recv, plane_send, plane_recv, back_send, back_recv,
    hop_send, hop_recv,
):
    g = lax.axis_index("grp")
    me = lax.axis_index("dev")
    yh, core = lax.div(g, 2), lax.rem(g, 2)
    x, yl, z = lax.div(me, 8), lax.rem(lax.div(me, 4), 2), lax.rem(me, 4)
    place = x * 4 + z
    other_half = (1 - yh) * 2
    across = x * 8 + (1 - yl) * 4 + z

    sibling = (yh * 2 + 1 - core, me)
    a_side = (g, across)
    b_side = (other_half + core, across)
    b_cross = (other_half + 1 - core, across)
    d_side = (other_half + core, me)

    def plane_peer(i):
        return lax.rem(x + lax.rem(i, 4), 4), lax.rem(z + i + lax.div(i, 4), 4)

    def columns(k):
        return pl.ds(sum(WIDTHS[:k]), WIDTHS[k])

    def remote(src, dst, send, recv, target):
        pltpu.make_async_remote_copy(
            src_ref=src, dst_ref=dst, send_sem=send, recv_sem=recv,
            device_id=target, device_id_type=MESH,
        ).start()

    order = list(range(CHUNKS))

    rows16 = pl.ds(pl.multiple_of(place * 16, 16), 16)
    pltpu.make_async_copy(light.at[yh, core, rows16], lbuf.at[0], light_recv).start()
    for k in order:
        pltpu.make_async_copy(
            grad.at[:, :, core, :, columns(k)], pbuf[k], load_sem.at[k]
        ).start()
    for k in order:
        pltpu.make_async_copy(field.at[:, :, columns(k)], obuf[k], field_sem.at[k]).start()

    barrier = pltpu.get_barrier_semaphore()
    for target in (sibling, a_side, b_side, b_cross, d_side):
        pl.semaphore_signal(barrier, 1, device_id=target, device_id_type=MESH)

    def greet(i, carry):
        px, pz = plane_peer(i)
        pl.semaphore_signal(
            barrier, 1, device_id=(g, px * 8 + yl * 4 + pz), device_id_type=MESH
        )
        return carry

    lax.fori_loop(1, 16, greet, 0)
    for half in range(2):
        mix_ref[half] = mixing_matrix(half)
    pl.semaphore_wait(barrier, 20)

    remote(light.at[yh, 1 - core, rows16], lbuf.at[1], light_send, light_recv, sibling)
    remote(light.at[1 - yh, core, rows16], lbuf.at[2], light_send, light_recv, b_side)
    remote(light.at[1 - yh, 1 - core, rows16], lbuf.at[3], light_send, light_recv, b_cross)

    for k in order:
        remote(
            grad.at[:, :, 1 - core, :, columns(k)], cbuf[k],
            core_send.at[k], core_recv.at[k], sibling,
        )

    mine = pl.ds(pl.multiple_of(yl * 128, 128), 128)
    theirs = pl.ds(pl.multiple_of((1 - yl) * 128, 128), 128)

    def damp_of(k, which):
        wide = dbuf.shape[-1]
        width = WIDTHS[k]
        half, start = sum(WIDTHS[:k]) // wide, sum(WIDTHS[:k]) % wide
        cols = slice(start, start + width)
        if which == "all":
            return dbuf[half, :, :, :, cols].reshape(256, width)
        if which == "mine":
            return dbuf[half, pl.ds(yl * 2, 2), :, :, cols].reshape(128, width)
        if which == "theirs":
            return dbuf[half, pl.ds((1 - yl) * 2, 2), :, :, cols].reshape(128, width)
        row = yl * 128 + place * 8
        return dbuf[half, lax.div(row, 64), lax.rem(lax.div(row, 16), 4),
                    pl.ds(pl.multiple_of(lax.rem(row, 16), 8), 8), cols]

    def chip_sum(k):
        wait_for(pbuf[k], load_sem.at[k])
        wait_for(cbuf[k], core_recv.at[k])
        pbuf[k][...] = pbuf[k][...] + cbuf[k][...]

    def early_d_send(k):
        remote(pbuf[k].at[:, 1 - yh, mine], from_d[k], y_send.at[0, k], y_recv.at[0, k], d_side)

    def early_b_send(k):
        remote(pbuf[k].at[:, 1 - yh, theirs], from_b[k], y_send.at[1, k], y_recv.at[1, k], b_side)

    def early_a_send(k):
        damp = damp_of(k, 'theirs')
        pbuf[k][:, yh, theirs] = obuf[k][:, theirs, :] * damp[None] - pbuf[k][:, yh, theirs]
        remote(pbuf[k].at[:, yh, theirs], from_a[k], y_send.at[2, k], y_recv.at[2, k], a_side)

    def ring(coordinate, i):
        return lax.rem(coordinate + i, 4)

    def reduce_damp():
        wait_for(lbuf, light_recv)
        total = lbuf[0] + lbuf[1] + lbuf[2] + lbuf[3] + damping
        wide = dbuf.shape[-1]
        for half in range(2):
            dbuf[half, x, z] = total[:, half * wide:(half + 1) * wide]
        for i in range(1, 4):
            remote(
                dbuf.at[0, x, z], dbuf.at[0, x, z], damp_send.at[0], damp_recv.at[0],
                (g, x * 8 + yl * 4 + ring(z, i)),
            )
            remote(
                dbuf.at[1, x, z], dbuf.at[1, x, z], damp_send.at[1], damp_recv.at[1],
                (g, ring(x, i) * 8 + yl * 4 + z),
            )

    def spread_damp():
        wait_for(dbuf.at[0, 0, pl.ds(0, 3)], damp_recv.at[0])
        for i in range(1, 4):
            remote(
                dbuf.at[0, x], dbuf.at[0, x], damp_send.at[2], damp_recv.at[2],
                (g, ring(x, i) * 8 + yl * 4 + z),
            )
        wait_for(dbuf.at[1, 0, pl.ds(0, 3)], damp_recv.at[1])
        for i in range(1, 4):
            remote(
                dbuf.at[1, :, z], dbuf.at[1, :, z], damp_send.at[3], damp_recv.at[3],
                (g, x * 8 + yl * 4 + ring(z, i)),
            )

    def wait_damp(half):
        wait_for(dbuf.at[half, pl.ds(0, 3)], damp_recv.at[2 + half])

    def mix(half, block):
        return jnp.dot(
            mix_ref[half], block, precision=lax.Precision.HIGHEST,
            preferred_element_type=jnp.float32,
        ).reshape(16, 8, block.shape[1])

    def early_plane(k):
        damp = damp_of(k, 'mine')
        wait_for(from_d[k], y_recv.at[0, k])
        sbuf[k][:, yl] = obuf[k][:, mine, :] * damp[None] - pbuf[k][:, yh, mine] - from_d[k][...]
        wait_for(from_b[k], y_recv.at[1, k])
        wait_for(from_a[k], y_recv.at[2, k])
        sbuf[k][:, 1 - yl] = from_a[k][...] - from_b[k][...]

        def send(i, carry):
            px, pz = plane_peer(i)
            rows = pl.ds(pl.multiple_of((px * 4 + pz) * 8, 8), 8)
            remote(
                sbuf[k].at[:, :, rows], xbuf[k].at[:, x, :, z], plane_send.at[k], plane_recv.at[k],
                (g, px * 8 + yl * 4 + pz),
            )
            return carry

        lax.fori_loop(1, 16, send, 0)
        own = pl.ds(pl.multiple_of(place * 8, 8), 8)
        pltpu.make_async_copy(
            sbuf[k].at[:, :, own], xbuf[k].at[:, x, :, z], plane_recv.at[k]
        ).start()

    def early_mix(k):
        wait_for(xbuf[k], plane_recv.at[k])
        inverse = 1.0 / damp_of(k, 'early')
        for half in range(2):
            real, imag = (
                mix(half, xbuf[k][part].reshape(256, WIDTHS[k])) * inverse[None] for part in range(2)
            )
            amplitude = jnp.sqrt(real * real + imag * imag)
            factor = ceiling / jnp.maximum(amplitude, ceiling)
            real, imag = real * factor, imag * factor
            ybuf[k][0, half] = real
            ybuf[k][1, half] = imag

    def early_return(k):
        rows = pl.ds(pl.multiple_of(place * 8, 8), 8)

        def send(i, carry):
            px, pz = plane_peer(i)
            remote(
                ybuf[k].at[:, :, px * 4 + pz], rbuf[k].at[:, :, rows], back_send.at[k], back_recv.at[k],
                (g, px * 8 + yl * 4 + pz),
            )
            return carry

        lax.fori_loop(1, 16, send, 0)
        pltpu.make_async_copy(
            ybuf[k].at[:, :, place], rbuf[k].at[:, :, rows], back_recv.at[k]
        ).start()

    def hop(k):
        wait_for(rbuf[k], back_recv.at[k])
        remote(
            rbuf[k].at[:, 1 - yl], out.at[:, mine, columns(k)], hop_send.at[k], hop_recv.at[k], a_side
        )
        pltpu.make_async_copy(
            rbuf[k].at[:, yl], out.at[:, mine, columns(k)], hop_recv.at[k]
        ).start()

    steps = {
        "sum": chip_sum, "ed": early_d_send, "eb": early_b_send, "ea": early_a_send,
        "dr": lambda k: reduce_damp(), "damp": lambda k: spread_damp(), "wd": wait_damp,
        "ep": early_plane, "em": early_mix, "er": early_return, "hop": hop,
        "wf": lambda k: wait_for(obuf[k], field_sem.at[k]),
    }
    for name, k in PLAN:
        steps[name](k)

    wait_for(lbuf.at[pl.ds(0, 3)], light_send)
    wait_for(dbuf.at[0, 0, pl.ds(0, 3)], damp_send.at[0])
    wait_for(dbuf.at[0, 0, pl.ds(0, 3)], damp_send.at[1])
    wait_for(dbuf.at[0, pl.ds(0, 3)], damp_send.at[2])
    wait_for(dbuf.at[0, pl.ds(0, 3)], damp_send.at[3])
    for k in range(CHUNKS):
        wait_for(cbuf[k], core_send.at[k])
        wait_for(from_d[k], y_send.at[0, k])
        wait_for(from_b[k], y_send.at[1, k])
        wait_for(from_a[k], y_send.at[2, k])
        wait_for(sbuf[k].at[:, :, pl.ds(0, 120)], plane_send.at[k])
        wait_for(rbuf[k].at[:, :, pl.ds(0, 120)], back_send.at[k])
        wait_for(rbuf[k].at[:, 0], hop_send.at[k])
        wait_for(out.at[:, :, columns(k)], hop_recv.at[k])


def per_device(grad_parts, light_parts, object_field):
    rows, columns = light_parts.shape[1:]
    slices = 32
    quarter = rows // 4
    half = quarter // 2
    f32 = jnp.float32
    grad = grad_parts.reshape(2, 2, 2, quarter, columns)
    light = light_parts.reshape(2, 2, quarter, columns)
    field = object_field.reshape(2, quarter, columns)
    in_hbm = pl.BlockSpec(memory_space=pltpu.HBM)
    in_vmem = pl.BlockSpec(memory_space=pltpu.VMEM)
    dma = pltpu.SemaphoreType.DMA

    def per_chunk(*shape):
        return tuple(pltpu.VMEM((*shape, width), f32) for width in WIDTHS)

    updated = pl.pallas_call(
        kernel,
        out_shape=jax.ShapeDtypeStruct((2, quarter, columns), f32),
        in_specs=[in_hbm] * 3,
        out_specs=in_vmem,
        scratch_shapes=[
            pltpu.VMEM((2, 128, 256), f32),
            per_chunk(2, 2, quarter),
            per_chunk(2, 2, quarter),
            per_chunk(2, quarter),
            pltpu.VMEM((4, 16, columns), f32),
            pltpu.VMEM((2, 4, 4, quarter // 16, columns // 2), f32),
            per_chunk(2, half),
            per_chunk(2, half),
            per_chunk(2, half),
            per_chunk(2, 2, half),
            per_chunk(2, 4, 2, 4, 8),
            per_chunk(2, 2, slices // 2, 8),
            per_chunk(2, 2, half),
            dma((CHUNKS,)), dma((CHUNKS,)),
            dma((CHUNKS,)), dma((CHUNKS,)),
            dma, dma,
            dma((4,)), dma((4,)),
            dma((3, CHUNKS)), dma((3, CHUNKS)),
            dma((CHUNKS,)), dma((CHUNKS,)),
            dma((CHUNKS,)), dma((CHUNKS,)),
            dma((CHUNKS,)), dma((CHUNKS,)),
        ],
        compiler_params=pltpu.CompilerParams(
            collective_id=0, has_side_effects=True, vmem_limit_bytes=51 * 2**20
        ),
    )(grad, light, field)
    return updated.reshape(object_field.shape)


def solution(mesh):
    in_specs = (
        P("grp", None, "dev", None, None),
        P("grp", None, None),
        P(None, "dev", "grp", None),
    )
    out_specs = P(None, "dev", "grp", None)
    return jax.shard_map(
        per_device, mesh=mesh, in_specs=in_specs, out_specs=out_specs, check_vma=False
    )
```
